256 devices in a mesh: wide: 32 (over x_hi, z, core), depth: 8 (over y, x_lo).
Axes of the slice: x: 4 (x_hi: 2, x_lo: 2; x = x_hi * 2 + x_lo), y: 4, z: 8, core: 2. Of those that a mesh axis runs over, the one named last changes fastest.
Arguments:
- schur: float32 [32, 8, 1536, 1536], P('wide', 'depth'), as said below
- loads: float32 [32, 8, 1536, 128], P('wide', 'depth'), may hold values from -6 to 6
- face_sizes: int32 [32, 8, 6], P('wide', 'depth'), may hold values from 64 to 256, as said below
- face_dir: int32 [32, 8, 6], P('wide', 'depth'), may hold values from 0 to 5, as said below
Outputs:
- displacement: float32 [32, 8, 1536, 128], P('wide', 'depth')
- residual: float32 [32, 8, 1536, 128], P('wide', 'depth')
The draws below stay inside these ranges and needn't reach their ends.
Inputs may be any that keep to these rules, and one draw needn't show every extreme that they name: `face_sizes`: A face slot and the neighbour's slot facing back across the same face have the same size; some slot holds 256 used unknowns and some holds 64. `face_dir`: each subdomain's six entries are 0 to 5 in some order: 0 faces the lower neighbour along wide, 1 the upper one, 2 the lower neighbour along depth, 3 the upper one, 4 and 5 the supported top and bottom surfaces. `schur`: each subdomain's matrix is symmetric and positive definite.
All inputs are finite; a program needn't handle non-finite values.
Results may differ from the reference program's by a relative error of at most 0.00017.
Values sent between devices are 32-bit elements; how exact they have to be, the bound alone decides.
A program may use at most 128 MiB of HBM per device.

```python
import jax
import jax.numpy as jnp
from jax import lax

FCAP = 256
NRHS = 128
ITERS = 2
M = 1536
GRID_W = 32
GRID_D = 8


def face_tables(key):
    first, second = jax.random.split(jax.random.fold_in(key, 7))
    base = jax.random.randint(first, (GRID_W, GRID_D, 6), FCAP // 4, FCAP + 1).astype(jnp.int32)
    base = base.at[0, 0, 4].set(FCAP).at[0, 0, 5].set(FCAP // 4)
    lower_w = jnp.concatenate([base[:1, :, 0], base[:-1, :, 1]], axis=0)
    lower_d = jnp.concatenate([base[:, :1, 2], base[:, :-1, 3]], axis=1)
    sized = jnp.stack([lower_w, base[..., 1], lower_d, base[..., 3], base[..., 4], base[..., 5]], axis=-1)
    scores = jax.random.randint(second, (GRID_W, GRID_D, 6), 0, 1000).astype(jnp.int32) * 6 + jnp.arange(6, dtype=jnp.int32)
    order = jnp.argsort(scores, axis=-1).astype(jnp.int32)
    slot_sizes = jnp.take_along_axis(sized, order, axis=-1).astype(jnp.int32)
    return (slot_sizes, order)


def draw_face_sizes(key, part):
    return face_tables(key)[0]


def draw_face_dir(key, part):
    return face_tables(key)[1]


def draw_schur(key, part):
    first, second, third = jax.random.split(jax.random.fold_in(key, 11), 3)
    noise = jax.random.normal(first, (GRID_W, GRID_D, M, M), jnp.float32)
    sym = (noise + jnp.swapaxes(noise, -1, -2)) * (0.5 / jnp.sqrt(2.0 * M))
    diag = jax.random.uniform(second, (GRID_W, GRID_D, M), jnp.float32, 1.5, 3.0)
    places = jnp.arange(FCAP, dtype=jnp.float32)
    kernel = jnp.exp(-jnp.abs(places[:, None] - places[None, :]) / (FCAP / 4.0))
    banded = (jnp.eye(6, dtype=jnp.float32)[:, None, :, None] * kernel[None, :, None, :]).reshape(M, M)
    amplitude = jax.random.uniform(third, (GRID_W, GRID_D, 6), jnp.float32, 0.06, 0.14)
    rooted = jnp.repeat(jnp.sqrt(amplitude), FCAP, axis=-1)
    smooth = rooted[..., :, None] * banded * rooted[..., None, :]
    return sym + diag[..., None] * jnp.eye(M, dtype=jnp.float32) + smooth


def level_of(own_key, dims, cuts, low, largest):
    def one(dim, blocks):
        heights = jax.random.uniform(jax.random.fold_in(jax.random.fold_in(own_key, 6), dim), (blocks,), jnp.float32, low / len(cuts), largest / len(cuts))
        return jnp.repeat(jnp.exp(heights), dims[dim] // blocks).reshape((-1,) + (1,) * (len(dims) - dim - 1))

    loudness = one(*cuts[0])
    for cut in cuts[1:]:
        loudness = loudness * one(*cut)
    return loudness


def scatter_about(own_key, shape, spread, most, cuts=(), kind=jnp.bfloat16):
    result = spread * jax.random.normal(own_key, shape, jnp.float32)
    if cuts:
        result = result * level_of(own_key, shape, cuts, -0.22, 0.18)
    return jnp.clip(result, -most, most).astype(kind)


def setup_inputs(seed: int = 0) -> dict:
    streams_of = jax.random.split(jax.random.key(seed), 5)
    return {
        "schur": draw_schur(jax.random.fold_in(streams_of[4], 71), 0),
        "loads": scatter_about(streams_of[1], (GRID_W, GRID_D, M, NRHS), 1.0, 6.0, ((0, 32), (1, 8)), jnp.float32),
        "face_sizes": draw_face_sizes(jax.random.fold_in(streams_of[4], 71), 0),
        "face_dir": draw_face_dir(jax.random.fold_in(streams_of[4], 71), 0),
    }


OMEGA = 0.6

def to_dirs(select, x):
    return jnp.einsum('...kd,...kfr->...dfr', select, x, precision=lax.Precision.HIGHEST)

def to_slots(select, x):
    return jnp.einsum('...kd,...dfr->...kfr', select, x, precision=lax.Precision.HIGHEST)

def assemble(select, parts):
    facing = to_dirs(select, parts)
    blank_w = jnp.zeros_like(facing[:1, :, 0])
    blank_d = jnp.zeros_like(facing[:, :1, 0])
    from_lower_w = jnp.concatenate([blank_w, facing[:-1, :, 1]], axis=0)
    from_upper_w = jnp.concatenate([facing[1:, :, 0], blank_w], axis=0)
    from_lower_d = jnp.concatenate([blank_d, facing[:, :-1, 3]], axis=1)
    from_upper_d = jnp.concatenate([facing[:, 1:, 2], blank_d], axis=1)
    blank = jnp.zeros_like(facing[:, :, 0])
    arrived = jnp.stack([from_lower_w, from_upper_w, from_lower_d, from_upper_d, blank, blank], axis=2)
    return parts + to_slots(select, arrived)

def reference(schur, loads, face_sizes, face_dir):
    slot_rows = FCAP
    cases = loads.shape[-1]
    mask = (jnp.arange(slot_rows, dtype=jnp.int32)[None, None, None, :] < face_sizes[..., None]).astype(jnp.float32)
    select = (face_dir[..., :, None] == jnp.arange(6, dtype=jnp.int32)).astype(jnp.float32)
    shaped = schur.reshape(GRID_W, GRID_D, 6, slot_rows, 6, slot_rows)
    blocks = jnp.stack([shaped[:, :, k, :, k, :] for k in range(6)], axis=2)
    summed = assemble(select, blocks)
    ident = jnp.eye(slot_rows, dtype=jnp.float32)
    summed = summed * mask[..., :, None] * mask[..., None, :] + ident * (1.0 - mask[..., :, None])
    factor = jnp.linalg.cholesky(summed)
    inverse = jax.scipy.linalg.cho_solve((factor, True), jnp.broadcast_to(ident, summed.shape))
    flat_schur = schur.reshape(GRID_W * GRID_D, M, M)

    def partial_value(disp):
        flat = disp.reshape(GRID_W * GRID_D, M, cases)
        applied = lax.map(lambda pair: jnp.dot(pair[0], pair[1], precision=lax.Precision.HIGHEST), (flat_schur, flat))
        local = loads - applied.reshape(GRID_W, GRID_D, M, cases)
        return local.reshape(GRID_W, GRID_D, 6, slot_rows, cases) * mask[..., None]
    disp = jnp.zeros((GRID_W, GRID_D, 6, slot_rows, cases), jnp.float32)
    for step in range(ITERS):
        resid = assemble(select, partial_value(disp))
        update = jnp.einsum('...fg,...gc->...fc', inverse, resid, precision=lax.Precision.HIGHEST)
        disp = disp + OMEGA * update
    final = assemble(select, partial_value(disp))
    return (disp.reshape(GRID_W, GRID_D, M, cases), final.reshape(GRID_W, GRID_D, M, cases))
```

```python
import functools

import jax
import jax.numpy as jnp
from jax import lax
from jax.experimental import pallas as pl
from jax.experimental.pallas import tpu as pltpu
from jax.sharding import PartitionSpec as P

OMEGA = 0.6
MESH = pl.DeviceIdType.MESH
F32 = jnp.float32
BF16 = jnp.bfloat16

ORDER = (2, 3, 0, 1, 4, 5)
FACES = 6
ROWS = 256
HALF = 128
BLOCK = 32


def split(x):
    high = x.astype(BF16)
    return high, (x - high.astype(F32)).astype(BF16)


def mm(a, b):
    ah, al = split(a)
    bh, bl = split(b)
    w = jnp.concatenate([bh, bl], 1)
    o = jnp.dot(jnp.concatenate([ah, al], 1), jnp.concatenate([w, w], 0), preferred_element_type=F32)
    return o[:, :HALF] + o[:, HALF:]


def row(x, i):
    return jnp.broadcast_to(x[i:i + 1], (8, HALF))


def packed_inverse(groups):
    tiles = BLOCK // 8
    lane = lax.broadcasted_iota(jnp.int32, (8, HALF), 1)
    sub = lax.broadcasted_iota(jnp.int32, (8, HALF), 0)
    seg = lane & 96
    within = lane & 31
    parts = [[g[8 * t:8 * t + 8] for t in range(tiles)] for g in groups]
    for m in range(tiles):
        inside = (within >> 3) == m
        cols = []
        for part in parts:
            cols.append([[jnp.take_along_axis(x, seg + (8 * m + k), axis=1) for x in part] for k in range(8)])
            for t in range(tiles):
                ident = (within == sub + 8 * t).astype(F32)
                part[t] = jnp.where(inside, ident, part[t])
        for i in range(8):
            here = sub == i
            for part, c in zip(parts, cols):
                rp = 1.0 / row(c[i][m], i)
                rn = row(part[m], i) * rp
                for k in range(i + 1, 8):
                    f = row(c[k][m], i) * rp
                    for t in range(tiles):
                        u = c[k][t] - c[i][t] * f
                        c[k][t] = jnp.where(here, f, u) if t == m else u
                for t in range(tiles):
                    u = part[t] - c[i][t] * rn
                    part[t] = jnp.where(here, rn, u) if t == m else u
    return [jnp.concatenate(part, 0) for part in parts]


def invert_halves(ref):
    count = ref.shape[0]
    groups = [list(range(g, min(g + 4, count))) for g in range(0, count, 4)]

    def body(s, carry):
        lane = lax.broadcasted_iota(jnp.int32, (BLOCK, HALF), 1)
        lanes = lax.broadcasted_iota(jnp.int32, (HALF, HALF), 1)
        sub = lax.broadcasted_iota(jnp.int32, (BLOCK, HALF), 0)
        here = pl.ds(pl.multiple_of(s * BLOCK, BLOCK), BLOCK)
        ident = ((lane & 31) == sub).astype(F32)
        packs, panels = [], []
        for group in groups:
            pack, panel = ident, []
            for i in group:
                active = (lane >> 5) == ((i + s) & 3)
                r = ref[i, here, :]
                pack = jnp.where(active, r, pack)
                panel.append(jnp.where(active, ident, r))
            packs.append(pack)
            panels.append(panel)
        inverses = packed_inverse(packs)
        for group, inverse, panel in zip(groups, inverses, panels):

            def by_segment(blocks):
                out = []
                for b in range(4):
                    x = jnp.zeros((BLOCK, HALF), F32)
                    for block, i in zip(blocks, group):
                        x = jnp.where(((i + s) & 3) == b, block, x)
                    out.append(x)
                return jnp.concatenate(out, 0)

            left = jnp.concatenate([jnp.where((lane >> 5) == ((i + s) & 3), inverse, 0.0) for i in group], 0)
            rn = mm(left, by_segment(panel))
            rns = [rn[BLOCK * x:BLOCK * x + BLOCK] for x in range(len(group))]
            cs, rests = [], []
            for i in group:
                active = (lanes >> 5) == ((i + s) & 3)
                m = ref[i]
                cs.append(jnp.where(active, m, 0.0))
                rests.append(jnp.where(active, 0.0, m))
            o = mm(jnp.concatenate(cs, 0), by_segment(rns))
            for x, i in enumerate(group):
                ref[i] = rests[x] - o[HALF * x:HALF * x + HALF]
                ref[i, here, :] = rns[x]
        return carry

    lax.fori_loop(0, HALF // BLOCK, body, 0)


def rotate(x, i):
    return x if i % 4 == 0 else pltpu.roll(x, BLOCK * (i % 4), 1)


def kernel(grid, schur, loads, sizes, dirs, disp_out, resid_out,
           full, diag, load, piece, got_piece, load_send, got_load, face, got_face, sh, sl, top, low, cross,
           ih, il, u, uu, acc, out_disp, out_resid,
           dma, full_s, piece_s, piece_r, load_s, load_r, face_s, face_r):
    wide, depth = lax.axis_index("wide"), lax.axis_index("depth")
    exists = (depth > 0, depth < grid[1] - 1, wide > 0, wide < grid[0] - 1)
    device = ((wide, depth - 1), (wide, depth + 1), (wide - 1, depth), (wide + 1, depth))

    fetch_diag = []
    for k in range(FACES):
        fetch_diag.append(pltpu.make_async_copy(
            schur.at[0, 0, pl.ds(k * ROWS, ROWS), pl.ds(k * ROWS, ROWS)], diag.at[k], dma.at[k]))
        fetch_diag[-1].start()
    fetch_load = []
    for k in range(FACES):
        fetch_load.append(pltpu.make_async_copy(
            loads.at[0, 0, pl.ds(k * ROWS, ROWS), :], load.at[k], dma.at[6 + k]))
        fetch_load[-1].start()
    fetch_full = []
    for k in range(FACES):
        for e in range(FACES):
            fetch_full.append(pltpu.make_async_copy(
                schur.at[0, 0, pl.ds(k * ROWS, ROWS), pl.ds(e * ROWS, ROWS)], full.at[k, e], full_s.at[k, e]))
            fetch_full[-1].start()

    barrier = pltpu.get_barrier_semaphore()
    for i in range(4):
        @pl.when(exists[i])
        def _(i=i):
            pl.semaphore_signal(barrier, inc=1, device_id=device[i], device_id_type=MESH)

    def slot_of(direction):
        k = jnp.int32(0)
        for x in range(1, FACES):
            k = jnp.where(dirs[0, 0, x] == direction, jnp.int32(x), k)
        return k

    slot = [slot_of(d) for d in ORDER]
    size = []
    for d in ORDER:
        n = sizes[0, 0, 0]
        for x in range(1, FACES):
            n = jnp.where(dirs[0, 0, x] == d, sizes[0, 0, x], n)
        size.append(n)

    def remote(buffer, into, send, recv, i, index):
        return pltpu.make_async_remote_copy(
            src_ref=buffer.at[(*index, i)], dst_ref=into.at[(*index, i ^ 1)],
            send_sem=send.at[(*index, i)], recv_sem=recv.at[(*index, i ^ 1)],
            device_id=device[i], device_id_type=MESH)

    def start(buffer, into, send, recv, i, index):
        @pl.when(exists[i])
        def _():
            remote(buffer, into, send, recv, i, index).start()

    def arrived(buffer, into, send, recv, i, index):
        @pl.when(exists[i])
        def _():
            pltpu.make_async_remote_copy(
                src_ref=buffer.at[(*index, i)], dst_ref=into.at[(*index, i)],
                send_sem=send.at[(*index, i)], recv_sem=recv.at[(*index, i)],
                device_id=device[i], device_id_type=MESH).wait_recv()

    def sent(buffer, into, send, recv, i, index):
        @pl.when(exists[i])
        def _():
            remote(buffer, into, send, recv, i, index).wait_send()

    pieces = (piece, got_piece, piece_s, piece_r)
    firsts = (load_send, got_load, load_s, load_r)
    faces = (face, got_face, face_s, face_r)

    for i in range(4):
        @pl.when(jnp.logical_not(exists[i]))
        def _(i=i):
            for j in range(3):
                got_piece[j, i] = jnp.zeros((HALF, HALF), F32)
            got_load[i] = jnp.zeros((ROWS, HALF), F32)
            for j in range(2):
                got_face[j, i] = jnp.zeros((ROWS, HALF), F32)

    for c in fetch_diag:
        c.wait()
    parts = ((0, 0), (HALF, 0), (HALF, HALF))
    for i in range(4):
        for j, (r, c) in enumerate(parts):
            piece[j, i] = diag[slot[i], pl.ds(r, HALF), pl.ds(c, HALF)]

    count = jnp.int32(0)
    for e in exists:
        count = count + jnp.where(e, jnp.int32(1), jnp.int32(0))
    pl.semaphore_wait(barrier, count)
    for j in range(3):
        for i in range(4):
            start(*pieces, i, (j,))
    for c in fetch_load:
        c.wait()
    rowid = lax.broadcasted_iota(jnp.int32, (ROWS, HALF), 0)

    def masked(x, i):
        return jnp.where(rowid < size[i], x, 0.0)

    for i in range(FACES):
        x = masked(load[slot[i]], i)
        acc[i] = x
        if i < 4:
            load_send[i] = x
    for i in range(4):
        start(*firsts, i, ())

    for c in fetch_full:
        c.wait()
    for i in range(FACES):
        for e in range(FACES):
            x = full[slot[i], slot[e]]
            h, l = split(x)
            sh[pl.ds(i * ROWS, ROWS), pl.ds(e * ROWS, ROWS)] = h
            sl[pl.ds(i * ROWS, ROWS), pl.ds(e * ROWS, ROWS)] = l

    hr = lax.broadcasted_iota(jnp.int32, (HALF, HALF), 0)
    hc = lax.broadcasted_iota(jnp.int32, (HALF, HALF), 1)

    def assembled(j, i):
        r, c = parts[j]
        x = diag[slot[i], pl.ds(r, HALF), pl.ds(c, HALF)]
        if i < 4:
            arrived(*pieces, i, (j,))
            x = x + got_piece[j, i]
        x = jnp.where((hr + r < size[i]) & (hc + c < size[i]), x, 0.0)
        if r == c:
            x = jnp.where((hr == hc) & (hr + r >= size[i]), 1.0, x)
        return x

    for i in range(FACES):
        top[i] = rotate(assembled(0, i), i)
    invert_halves(top)
    for i in range(FACES):
        p = rotate(top[i], -i)
        top[i] = p
        b = assembled(1, i)
        w = mm(b, p)
        cross[i] = w
        low[i] = rotate(assembled(2, i) - mm(w, b.T), i)
    invert_halves(low)
    for i in range(FACES):
        w = cross[i]
        q = rotate(low[i], -i)
        v = -mm(q, w)
        for r, c, x in ((0, 0, top[i] - mm(w.T, v)), (HALF, 0, v), (0, HALF, v.T), (HALF, HALF, q)):
            h, l = split(x)
            ih[i, pl.ds(r, HALF), pl.ds(c, HALF)] = h
            il[i, pl.ds(r, HALF), pl.ds(c, HALF)] = l

    def solve(i, r):
        h, l = split(r)
        w = jnp.concatenate([h, l], 1)
        o = jnp.dot(ih[i], w, preferred_element_type=F32) + jnp.dot(il[i], w, preferred_element_type=F32)
        return OMEGA * (o[:, :HALF] + o[:, HALF:])

    def keep(i, x):
        u[i] = x
        h, l = split(x)
        uu[pl.ds(i * ROWS, ROWS), pl.ds(0, HALF)] = h
        uu[pl.ds(i * ROWS, ROWS), pl.ds(HALF, HALF)] = l

    def applied(i, begin, end):
        rows, cols = pl.ds(i * ROWS, ROWS), pl.ds(begin * ROWS, (end - begin) * ROWS)
        w = uu[cols, :]
        o = jnp.dot(sh[rows, cols], w, preferred_element_type=F32) + jnp.dot(sl[rows, cols], w, preferred_element_type=F32)
        return o[:, :HALF] + o[:, HALF:]

    for i in range(FACES):
        r = acc[i]
        if i < 4:
            arrived(*firsts, i, ())
            r = r + got_load[i]
        keep(i, solve(i, r))
    for i in range(FACES):
        x = acc[i] - masked(applied(i, 0, FACES), i)
        face[0, i] = x
        if i < 4:
            start(*faces, i, (0,))

    for i in (4, 5, 2, 3):
        r = face[0, i]
        if i < 4:
            arrived(*faces, i, (0,))
            r = r + got_face[0, i]
        keep(i, u[i] + solve(i, r))
    for i in range(FACES):
        acc[i] = acc[i] - masked(applied(i, 2, FACES), i)
    for i in (0, 1):
        arrived(*faces, i, (0,))
        keep(i, u[i] + solve(i, face[0, i] + got_face[0, i]))
    for i in range(FACES):
        x = acc[i] - masked(applied(i, 0, 2), i)
        face[1, i] = x
        if i < 4:
            start(*faces, i, (1,))

    def place(k):
        d = dirs[0, 0, k]
        return jnp.where(d < 2, d + 2, jnp.where(d < 4, d - 2, d))

    for k in range(FACES):
        out_disp[pl.ds(k * ROWS, ROWS), :] = u[place(k)]
    give_disp = pltpu.make_async_copy(out_disp, disp_out.at[0, 0], dma.at[12])
    give_disp.start()
    for i in (4, 5, 2, 3, 0, 1):
        x = face[1, i]
        if i < 4:
            arrived(*faces, i, (1,))
            x = x + got_face[1, i]
        acc[i] = x
    for k in range(FACES):
        out_resid[pl.ds(k * ROWS, ROWS), :] = acc[place(k)]
    give_resid = pltpu.make_async_copy(out_resid, resid_out.at[0, 0], dma.at[13])
    give_resid.start()
    for i in range(4):
        for j in range(3):
            sent(*pieces, i, (j,))
        sent(*firsts, i, ())
        for j in range(2):
            sent(*faces, i, (j,))
    give_disp.wait()
    give_resid.wait()


def solution(mesh):
    grid = (mesh.shape["wide"], mesh.shape["depth"])

    def local(schur, loads, face_sizes, face_dir):
        order, cases = schur.shape[2], loads.shape[3]
        shape = jax.ShapeDtypeStruct((1, 1, order, cases), F32)
        hbm = pl.BlockSpec(memory_space=pl.ANY)
        smem = pl.BlockSpec(memory_space=pltpu.SMEM)
        vmem = pltpu.VMEM
        sem = pltpu.SemaphoreType.DMA
        return pl.pallas_call(
            functools.partial(kernel, grid),
            out_shape=(shape, shape),
            in_specs=[hbm, hbm, smem, smem],
            out_specs=(hbm, hbm),
            scratch_shapes=[
                vmem((FACES, FACES, ROWS, ROWS), F32),
                vmem((FACES, ROWS, ROWS), F32),
                vmem((FACES, ROWS, HALF), F32),
                vmem((3, 4, HALF, HALF), F32),
                vmem((3, 4, HALF, HALF), F32),
                vmem((4, ROWS, HALF), F32),
                vmem((4, ROWS, HALF), F32),
                vmem((2, FACES, ROWS, HALF), F32),
                vmem((2, 4, ROWS, HALF), F32),
                vmem((order, order), BF16),
                vmem((order, order), BF16),
                vmem((FACES, HALF, HALF), F32),
                vmem((FACES, HALF, HALF), F32),
                vmem((FACES, HALF, HALF), F32),
                vmem((FACES, ROWS, ROWS), BF16),
                vmem((FACES, ROWS, ROWS), BF16),
                vmem((FACES, ROWS, HALF), F32),
                vmem((order, ROWS), BF16),
                vmem((FACES, ROWS, HALF), F32),
                vmem((order, cases), F32),
                vmem((order, cases), F32),
                sem((14,)),
                sem((FACES, FACES)),
                sem((3, 4)),
                sem((3, 4)),
                sem((4,)),
                sem((4,)),
                sem((2, 4)),
                sem((2, 4)),
            ],
            compiler_params=pltpu.CompilerParams(
                collective_id=0, has_side_effects=True, vmem_limit_bytes=56 << 20),
        )(schur, loads, face_sizes, face_dir)

    return jax.shard_map(
        local,
        mesh=mesh,
        in_specs=(
            P("wide", "depth", None, None),
            P("wide", "depth", None, None),
            P("wide", "depth", None),
            P("wide", "depth", None),
        ),
        out_specs=(P("wide", "depth", None, None), P("wide", "depth", None, None)),
        check_vma=False,
    )
```

```python
import functools

import jax
import jax.numpy as jnp
from jax import lax
from jax.experimental import pallas as pl
from jax.experimental.pallas import tpu as pltpu
from jax.sharding import PartitionSpec as P

OMEGA = 0.6
MESH = pl.DeviceIdType.MESH
F32 = jnp.float32
BF16 = jnp.bfloat16

ORDER = (2, 3, 0, 1, 4, 5)
FACES = 6
ROWS = 256
HALF = 128
BLOCK = 32


def split(x):
    high = x.astype(BF16)
    return high, (x - high.astype(F32)).astype(BF16)


def mm(a, b):
    ah, al = split(a)
    bh, bl = split(b)
    w = jnp.concatenate([bh, bl], 1)
    o = jnp.dot(jnp.concatenate([ah, al], 1), jnp.concatenate([w, w], 0), preferred_element_type=F32)
    return o[:, :HALF] + o[:, HALF:]


def row(x, i):
    return jnp.broadcast_to(x[i:i + 1], (8, HALF))


def packed_inverse(groups):
    tiles = BLOCK // 8
    lane = lax.broadcasted_iota(jnp.int32, (8, HALF), 1)
    sub = lax.broadcasted_iota(jnp.int32, (8, HALF), 0)
    seg = lane & 96
    within = lane & 31
    parts = [[g[8 * t:8 * t + 8] for t in range(tiles)] for g in groups]
    for m in range(tiles):
        inside = (within >> 3) == m
        cols = []
        for part in parts:
            cols.append([[jnp.take_along_axis(x, seg + (8 * m + k), axis=1) for x in part] for k in range(8)])
            for t in range(tiles):
                ident = (within == sub + 8 * t).astype(F32)
                part[t] = jnp.where(inside, ident, part[t])
        for i in range(8):
            here = sub == i
            for part, c in zip(parts, cols):
                rp = 1.0 / row(c[i][m], i)
                rn = row(part[m], i) * rp
                for k in range(i + 1, 8):
                    f = row(c[k][m], i) * rp
                    for t in range(tiles):
                        u = c[k][t] - c[i][t] * f
                        c[k][t] = jnp.where(here, f, u) if t == m else u
                for t in range(tiles):
                    u = part[t] - c[i][t] * rn
                    part[t] = jnp.where(here, rn, u) if t == m else u
    return [jnp.concatenate(part, 0) for part in parts]


def invert_halves(refs, beside=None):
    def body(s, carry):
        lane = lax.broadcasted_iota(jnp.int32, (BLOCK, HALF), 1)
        lanes = lax.broadcasted_iota(jnp.int32, (HALF, HALF), 1)
        sub = lax.broadcasted_iota(jnp.int32, (BLOCK, HALF), 0)
        here = pl.ds(pl.multiple_of(s * BLOCK, BLOCK), BLOCK)
        ident = ((lane & 31) == sub).astype(F32)
        packs = []
        for ref in refs:
            pack = ident
            for i in range(ref.shape[0]):
                pack = jnp.where((lane >> 5) == ((i + s) & 3), ref[i, here, :], pack)
            packs.append(pack)
        inverses = [packed_inverse([p])[0] for p in packs]
        if beside is not None:
            beside(s)
        for ref, inverse in zip(refs, inverses):
            count = ref.shape[0]

            def by_segment(blocks):
                out = []
                for b in range(4):
                    x = jnp.zeros((BLOCK, HALF), F32)
                    for i, block in enumerate(blocks):
                        x = jnp.where(((i + s) & 3) == b, block, x)
                    out.append(x)
                return jnp.concatenate(out, 0)

            active = [(lane >> 5) == ((i + s) & 3) for i in range(count)]
            left = jnp.concatenate([jnp.where(active[i], inverse, 0.0) for i in range(count)], 0)
            rn = mm(left, by_segment([jnp.where(active[i], ident, ref[i, here, :]) for i in range(count)]))
            rns = [rn[BLOCK * i:BLOCK * i + BLOCK] for i in range(count)]
            cs, rests = [], []
            for i in range(count):
                x = ref[i]
                mine = (lanes >> 5) == ((i + s) & 3)
                cs.append(jnp.where(mine, x, 0.0))
                rests.append(jnp.where(mine, 0.0, x))
            o = mm(jnp.concatenate(cs, 0), by_segment(rns))
            for i in range(count):
                ref[i] = rests[i] - o[HALF * i:HALF * i + HALF]
                ref[i, here, :] = rns[i]
        return carry

    lax.fori_loop(0, HALF // BLOCK, body, 0)


def rotate(x, i):
    return x if i % 4 == 0 else pltpu.roll(x, BLOCK * (i % 4), 1)


def kernel(grid, schur, loads, sizes, dirs, disp_out, resid_out,
           full, diag, load, corner, got_corner, piece, got_piece, load_send, got_load, face, got_face, both, top_a, top_b, low_a, low_b, cross,
           inv, u, uu, acc, out_disp, out_resid,
           dma, full_s, disp_s, resid_s, corner_s, corner_r, piece_s, piece_r, load_s, load_r, face_s, face_r):
    top, low = (top_a, top_b), (low_a, low_b)
    wide, depth = lax.axis_index("wide"), lax.axis_index("depth")
    exists = (depth > 0, depth < grid[1] - 1, wide > 0, wide < grid[0] - 1)
    device = ((wide, depth - 1), (wide, depth + 1), (wide - 1, depth), (wide + 1, depth))

    fetch_diag = []
    for k in range(FACES):
        fetch_diag.append(pltpu.make_async_copy(
            schur.at[0, 0, pl.ds(k * ROWS, ROWS), pl.ds(k * ROWS, ROWS)], diag.at[k], dma.at[k]))
        fetch_diag[-1].start()
    fetch_load = []
    for k in range(FACES):
        fetch_load.append(pltpu.make_async_copy(
            loads.at[0, 0, pl.ds(k * ROWS, ROWS), :], load.at[k], dma.at[6 + k]))
        fetch_load[-1].start()
    fetch_full = []
    for k in range(FACES):
        for e in range(FACES):
            fetch_full.append(pltpu.make_async_copy(
                schur.at[0, 0, pl.ds(k * ROWS, ROWS), pl.ds(e * ROWS, ROWS)], full.at[k, e], full_s.at[k, e]))
            fetch_full[-1].start()

    barrier = pltpu.get_barrier_semaphore()
    for i in range(4):
        @pl.when(exists[i])
        def _(i=i):
            pl.semaphore_signal(barrier, inc=1, device_id=device[i], device_id_type=MESH)

    def slot_of(direction):
        k = jnp.int32(0)
        for x in range(1, FACES):
            k = jnp.where(dirs[0, 0, x] == direction, jnp.int32(x), k)
        return k

    slot = [slot_of(d) for d in ORDER]
    size = []
    for d in ORDER:
        n = sizes[0, 0, 0]
        for x in range(1, FACES):
            n = jnp.where(dirs[0, 0, x] == d, sizes[0, 0, x], n)
        size.append(n)

    def remote(buffer, into, send, recv, i, index):
        return pltpu.make_async_remote_copy(
            src_ref=buffer.at[(*index, i)], dst_ref=into.at[(*index, i ^ 1)],
            send_sem=send.at[(*index, i)], recv_sem=recv.at[(*index, i ^ 1)],
            device_id=device[i], device_id_type=MESH)

    def start(buffer, into, send, recv, i, index):
        @pl.when(exists[i])
        def _():
            remote(buffer, into, send, recv, i, index).start()

    def arrived(buffer, into, send, recv, i, index):
        @pl.when(exists[i])
        def _():
            pltpu.make_async_remote_copy(
                src_ref=buffer.at[(*index, i)], dst_ref=into.at[(*index, i)],
                send_sem=send.at[(*index, i)], recv_sem=recv.at[(*index, i)],
                device_id=device[i], device_id_type=MESH).wait_recv()

    def sent(buffer, into, send, recv, i, index):
        @pl.when(exists[i])
        def _():
            remote(buffer, into, send, recv, i, index).wait_send()

    corners = (corner, got_corner, corner_s, corner_r)
    pieces = (piece, got_piece, piece_s, piece_r)
    firsts = (load_send, got_load, load_s, load_r)
    faces = (face, got_face, face_s, face_r)

    for i in range(4):
        @pl.when(jnp.logical_not(exists[i]))
        def _(i=i):
            got_corner[i] = jnp.zeros((HALF + 8, HALF), F32)
            got_piece[i] = jnp.zeros((HALF, HALF), F32)
            got_load[i] = jnp.zeros((ROWS, HALF), F32)
            for j in range(2):
                got_face[j, i] = jnp.zeros((ROWS, HALF), F32)

    for c in fetch_diag:
        c.wait()
    hr = lax.broadcasted_iota(jnp.int32, (HALF, HALF), 0)
    hc = lax.broadcasted_iota(jnp.int32, (HALF, HALF), 1)
    parts = ((0, 0), (HALF, 0), (HALF, HALF))

    def own(j, i):
        r, c = parts[j]
        return diag[slot[i], pl.ds(r, HALF), pl.ds(c, HALF)]

    for i in range(4):
        first, last = own(0, i), own(2, i)
        corner[i, pl.ds(0, HALF), :] = jnp.where(hc <= hr, first, last)
        middle = jnp.sum(jnp.where(hc == hr, last, 0.0), axis=0, keepdims=True)
        corner[i, pl.ds(HALF, 8), :] = jnp.broadcast_to(middle, (8, HALF))
        piece[i] = own(1, i)

    count = jnp.int32(0)
    for e in exists:
        count = count + jnp.where(e, jnp.int32(1), jnp.int32(0))
    pl.semaphore_wait(barrier, count)
    for i in range(4):
        start(*corners, i, ())
    for c in fetch_load:
        c.wait()
    rowid = lax.broadcasted_iota(jnp.int32, (ROWS, HALF), 0)

    def masked(x, i):
        return jnp.where(rowid < size[i], x, 0.0)

    for i in range(FACES):
        x = masked(load[slot[i]], i)
        acc[i] = x
        if i < 4:
            load_send[i] = x

    def convert(half, s):
        part = ROWS // 4
        begin = pl.multiple_of(s * part, part)
        for i in range(3 * half, 3 * half + 3):
            for e in range(FACES):
                h, l = split(full[slot[i], slot[e], pl.ds(begin, part), :])
                both[pl.ds(i * 2 * ROWS + begin, part), pl.ds(e * ROWS, ROWS)] = h
                both[pl.ds(i * 2 * ROWS + ROWS + begin, part), pl.ds(e * ROWS, ROWS)] = l

    def assembled(j, i):
        r, c = parts[j]
        if i >= 4:
            x = own(j, i)
        elif j == 1:
            arrived(*pieces, i, ())
            x = piece[i] + got_piece[i]
        else:
            if j == 0:
                arrived(*corners, i, ())
            x = corner[i, pl.ds(0, HALF), :] + got_corner[i, pl.ds(0, HALF), :]
            x = jnp.where(hc <= hr if j == 0 else hc > hr, x, 0.0)
            y = x.T
            if j == 0:
                x = jnp.where(hc > hr, y, x)
            else:
                middle = corner[i, pl.ds(HALF, 8), :] + got_corner[i, pl.ds(HALF, 8), :]
                x = jnp.where(hc == hr, jnp.broadcast_to(middle[:1], (HALF, HALF)), x + y)
        x = jnp.where((hr + r < size[i]) & (hc + c < size[i]), x, 0.0)
        if r == c:
            x = jnp.where((hr == hc) & (hr + r >= size[i]), 1.0, x)
        return x

    def at(pair, i):
        return pair[i // 4].at[i % 4]

    def halve(i):
        p = rotate(at(top, i)[...], -i)
        at(top, i)[...] = p
        b = assembled(1, i)
        w = mm(b, p)
        cross[i] = w
        at(low, i)[...] = rotate(assembled(2, i) - mm(w, b.T), i)

    for c in fetch_full:
        c.wait()
    for i in (4, 5, 2, 3, 0, 1):
        at(top, i)[...] = rotate(assembled(0, i), i)
    for i in range(4):
        start(*pieces, i, ())

    for i in range(4):
        start(*firsts, i, ())

    def beside_top(s):
        convert(0, s)


    invert_halves(top, beside_top)
    for i in (4, 5, 2, 3, 0, 1):
        halve(i)
    invert_halves(low, functools.partial(convert, 1))

    def first_solve(i, r):
        p, w, q = at(top, i)[...], cross[i], rotate(at(low, i)[...], -i)
        at(low, i)[...] = q
        upper, lower = r[:HALF], r[HALF:]
        y = mm(q, lower - mm(w, upper))
        return OMEGA * jnp.concatenate([mm(p, upper) - mm(w.T, y), y], 0)

    def explicit(i):
        w, q = cross[i], at(low, i)[...]
        v = -mm(q, w)
        for r, c, x in ((0, 0, at(top, i)[...] - mm(w.T, v)), (HALF, 0, v), (0, HALF, v.T), (HALF, HALF, q)):
            h, l = split(x)
            inv[i, pl.ds(r, HALF), pl.ds(c, HALF)] = h
            inv[i, pl.ds(ROWS + r, HALF), pl.ds(c, HALF)] = l

    def folded(o):
        return (o[:ROWS, :HALF] + o[:ROWS, HALF:]) + (o[ROWS:, :HALF] + o[ROWS:, HALF:])

    def solve(i, r):
        h, l = split(r)
        w = jnp.concatenate([h, l], 1)
        return OMEGA * folded(jnp.dot(inv[i], w, preferred_element_type=F32))

    def keep(i, x):
        u[i] = x
        h, l = split(x)
        uu[pl.ds(i * ROWS, ROWS), pl.ds(0, HALF)] = h
        uu[pl.ds(i * ROWS, ROWS), pl.ds(HALF, HALF)] = l

    def applied(i, begin, end):
        rows, cols = pl.ds(i * 2 * ROWS, 4 * ROWS), pl.ds(begin * ROWS, (end - begin) * ROWS)
        o = jnp.dot(both[rows, cols], uu[cols, :], preferred_element_type=F32)
        return masked(folded(o[:2 * ROWS]), i), masked(folded(o[2 * ROWS:]), i + 1)

    for i in range(FACES):
        r = acc[i]
        if i < 4:
            arrived(*firsts, i, ())
            r = r + got_load[i]
        keep(i, first_solve(i, r))
    for i in range(0, FACES, 2):
        for j, x in enumerate(applied(i, 0, FACES)):
            face[0, i + j] = acc[i + j] - x
            if i < 4:
                start(*faces, i + j, (0,))

    for i in (4, 5, 2, 3, 0, 1):
        explicit(i)

    for i in (4, 5, 2, 3):
        r = face[0, i]
        if i < 4:
            arrived(*faces, i, (0,))
            r = r + got_face[0, i]
        keep(i, u[i] + solve(i, r))
    for i in range(0, FACES, 2):
        for j, x in enumerate(applied(i, 2, FACES)):
            acc[i + j] = acc[i + j] - x
    for i in (0, 1):
        arrived(*faces, i, (0,))
        keep(i, u[i] + solve(i, face[0, i] + got_face[0, i]))
    for i in range(0, FACES, 2):
        for j, x in enumerate(applied(i, 0, 2)):
            face[1, i + j] = acc[i + j] - x
            if i < 4:
                start(*faces, i + j, (1,))

    def place(k):
        d = dirs[0, 0, k]
        return jnp.where(d < 2, d + 2, jnp.where(d < 4, d - 2, d))

    gives = []

    def give(k, x, held, out, sems):
        rows = pl.ds(k * ROWS, ROWS)
        held[rows, :] = x
        gives.append(pltpu.make_async_copy(held.at[rows, :], out.at[0, 0, rows, :], sems.at[k]))
        gives[-1].start()

    for k in range(FACES):
        give(k, u[place(k)], out_disp, disp_out, disp_s)
    for i in (4, 5, 2, 3, 0, 1):
        x = face[1, i]
        if i < 4:
            arrived(*faces, i, (1,))
            x = x + got_face[1, i]
        acc[i] = x
    for k in range(FACES):
        give(k, acc[place(k)], out_resid, resid_out, resid_s)
    for i in range(4):
        sent(*corners, i, ())
        sent(*pieces, i, ())
        sent(*firsts, i, ())
        for j in range(2):
            sent(*faces, i, (j,))
    for c in gives:
        c.wait()


def hand_over(disp, resid, disp_out, resid_out, held, sems):
    rows = disp.shape[2] // 3
    ins, outs = [], []
    for i, (a, b) in enumerate(((disp, disp_out), (resid, resid_out))):
        for k in range(3):
            part = pl.ds(k * rows, rows)
            ins.append(pltpu.make_async_copy(a.at[0, 0, part, :], held.at[i, k], sems.at[0, i, k]))
            outs.append(pltpu.make_async_copy(held.at[i, k], b.at[0, 0, part, :], sems.at[1, i, k]))
            ins[-1].start()
    for c, d in zip(ins, outs):
        c.wait()
        d.start()
    for d in outs:
        d.wait()


def solution(mesh):
    grid = (mesh.shape["wide"], mesh.shape["depth"])

    def local(schur, loads, face_sizes, face_dir):
        order, cases = schur.shape[2], loads.shape[3]
        shape = jax.ShapeDtypeStruct((1, 1, order, cases), F32)
        hbm = pl.BlockSpec(memory_space=pl.ANY)
        smem = pl.BlockSpec(memory_space=pltpu.SMEM)
        vmem = pltpu.VMEM
        sem = pltpu.SemaphoreType.DMA
        found = pl.pallas_call(
            functools.partial(kernel, grid),
            out_shape=(shape, shape),
            in_specs=[hbm, hbm, smem, smem],
            out_specs=(hbm, hbm),
            scratch_shapes=[
                vmem((FACES, FACES, ROWS, ROWS), F32),
                vmem((FACES, ROWS, ROWS), F32),
                vmem((FACES, ROWS, HALF), F32),
                vmem((4, HALF + 8, HALF), F32),
                vmem((4, HALF + 8, HALF), F32),
                vmem((4, HALF, HALF), F32),
                vmem((4, HALF, HALF), F32),
                vmem((4, ROWS, HALF), F32),
                vmem((4, ROWS, HALF), F32),
                vmem((2, FACES, ROWS, HALF), F32),
                vmem((2, 4, ROWS, HALF), F32),
                vmem((2 * order, order), BF16),
                vmem((4, HALF, HALF), F32),
                vmem((2, HALF, HALF), F32),
                vmem((4, HALF, HALF), F32),
                vmem((2, HALF, HALF), F32),
                vmem((FACES, HALF, HALF), F32),
                vmem((FACES, 2 * ROWS, ROWS), BF16),
                vmem((FACES, ROWS, HALF), F32),
                vmem((order, ROWS), BF16),
                vmem((FACES, ROWS, HALF), F32),
                vmem((order, cases), F32),
                vmem((order, cases), F32),
                sem((12,)),
                sem((FACES, FACES)),
                sem((FACES,)),
                sem((FACES,)),
                sem((4,)),
                sem((4,)),
                sem((4,)),
                sem((4,)),
                sem((4,)),
                sem((4,)),
                sem((2, 4)),
                sem((2, 4)),
            ],
            compiler_params=pltpu.CompilerParams(
                collective_id=0, has_side_effects=True, vmem_limit_bytes=56 << 20),
        )(schur, loads, face_sizes, face_dir)
        return tuple(pl.pallas_call(
            hand_over,
            out_shape=(shape, shape),
            in_specs=[hbm, hbm],
            out_specs=(hbm, hbm),
            scratch_shapes=[vmem((2, 3, order // 3, cases), F32), sem((2, 2, 3))],
        )(*found))

    return jax.shard_map(
        local,
        mesh=mesh,
        in_specs=(
            P("wide", "depth", None, None),
            P("wide", "depth", None, None),
            P("wide", "depth", None),
            P("wide", "depth", None),
        ),
        out_specs=(P("wide", "depth", None, None), P("wide", "depth", None, None)),
        check_vma=False,
    )
```

```python
import functools

import jax
import jax.numpy as jnp
from jax import lax
from jax.experimental import pallas as pl
from jax.experimental.pallas import tpu as pltpu
from jax.sharding import PartitionSpec as P

OMEGA = 0.6
MESH = pl.DeviceIdType.MESH
F32 = jnp.float32
BF16 = jnp.bfloat16

ORDER = (2, 3, 0, 1, 4, 5)
FACES = 6
ROWS = 256
HALF = 128
BLOCK = 32


def split(x):
    high = x.astype(BF16)
    return high, (x - high.astype(F32)).astype(BF16)


def mm(a, b):
    ah, al = split(a)
    bh, bl = split(b)
    w = jnp.concatenate([bh, bl], 1)
    o = jnp.dot(jnp.concatenate([ah, al], 1), jnp.concatenate([w, w], 0), preferred_element_type=F32)
    return o[:, :HALF] + o[:, HALF:]


def row(x, i):
    return jnp.broadcast_to(x[i:i + 1], (8, HALF))


def packed_inverse(groups):
    tiles = BLOCK // 8
    lane = lax.broadcasted_iota(jnp.int32, (8, HALF), 1)
    sub = lax.broadcasted_iota(jnp.int32, (8, HALF), 0)
    seg = lane & 96
    within = lane & 31
    parts = [[g[8 * t:8 * t + 8] for t in range(tiles)] for g in groups]
    for m in range(tiles):
        inside = (within >> 3) == m
        cols = []
        for part in parts:
            cols.append([[jnp.take_along_axis(x, seg + (8 * m + k), axis=1) for x in part] for k in range(8)])
            for t in range(tiles):
                ident = (within == sub + 8 * t).astype(F32)
                part[t] = jnp.where(inside, ident, part[t])
        for i in range(8):
            here = sub == i
            for part, c in zip(parts, cols):
                rp = 1.0 / row(c[i][m], i)
                rn = row(part[m], i) * rp
                for k in range(i + 1, 8):
                    f = row(c[k][m], i) * rp
                    for t in range(tiles):
                        u = c[k][t] - c[i][t] * f
                        c[k][t] = jnp.where(here, f, u) if t == m else u
                for t in range(tiles):
                    u = part[t] - c[i][t] * rn
                    part[t] = jnp.where(here, rn, u) if t == m else u
    return [jnp.concatenate(part, 0) for part in parts]


def invert_halves(refs, beside=None):
    def body(s, carry):
        lane = lax.broadcasted_iota(jnp.int32, (BLOCK, HALF), 1)
        lanes = lax.broadcasted_iota(jnp.int32, (HALF, HALF), 1)
        sub = lax.broadcasted_iota(jnp.int32, (BLOCK, HALF), 0)
        here = pl.ds(pl.multiple_of(s * BLOCK, BLOCK), BLOCK)
        ident = ((lane & 31) == sub).astype(F32)
        packs = []
        for ref in refs:
            pack = ident
            for i in range(ref.shape[0]):
                pack = jnp.where((lane >> 5) == ((i + s) & 3), ref[i, here, :], pack)
            packs.append(pack)
        inverses = [packed_inverse([p])[0] for p in packs]
        if beside is not None:
            beside(s)
        for ref, inverse in zip(refs, inverses):
            count = ref.shape[0]

            def by_segment(blocks):
                out = []
                for b in range(4):
                    x = jnp.zeros((BLOCK, HALF), F32)
                    for i, block in enumerate(blocks):
                        x = jnp.where(((i + s) & 3) == b, block, x)
                    out.append(x)
                return jnp.concatenate(out, 0)

            active = [(lane >> 5) == ((i + s) & 3) for i in range(count)]
            left = jnp.concatenate([jnp.where(active[i], inverse, 0.0) for i in range(count)], 0)
            rn = mm(left, by_segment([jnp.where(active[i], ident, ref[i, here, :]) for i in range(count)]))
            rns = [rn[BLOCK * i:BLOCK * i + BLOCK] for i in range(count)]
            cs, rests = [], []
            for i in range(count):
                x = ref[i]
                mine = (lanes >> 5) == ((i + s) & 3)
                cs.append(jnp.where(mine, x, 0.0))
                rests.append(jnp.where(mine, 0.0, x))
            o = mm(jnp.concatenate(cs, 0), by_segment(rns))
            for i in range(count):
                ref[i] = rests[i] - o[HALF * i:HALF * i + HALF]
                ref[i, here, :] = rns[i]
        return carry

    lax.fori_loop(0, HALF // BLOCK, body, 0)


def rotate(x, i):
    return x if i % 4 == 0 else pltpu.roll(x, BLOCK * (i % 4), 1)


def kernel(grid, schur, loads, sizes, dirs, disp_out, resid_out,
           full, diag, load, corner, got_corner, piece, got_piece, load_send, got_load, face, got_face, both, top_a, top_b, low_a, low_b, cross,
           inv, u, uu, acc, out_disp, out_resid,
           dma, full_s, disp_s, resid_s, corner_s, corner_r, piece_s, piece_r, load_s, load_r, face_s, face_r):
    top, low = (top_a, top_b), (low_a, low_b)
    wide, depth = lax.axis_index("wide"), lax.axis_index("depth")
    exists = (depth > 0, depth < grid[1] - 1, wide > 0, wide < grid[0] - 1)
    device = ((wide, depth - 1), (wide, depth + 1), (wide - 1, depth), (wide + 1, depth))

    fetch_diag = []
    for k in range(FACES):
        fetch_diag.append(pltpu.make_async_copy(
            schur.at[0, 0, pl.ds(k * ROWS, ROWS), pl.ds(k * ROWS, ROWS)], diag.at[k], dma.at[k]))
        fetch_diag[-1].start()
    barrier = pltpu.get_barrier_semaphore()
    for i in range(4):
        @pl.when(exists[i])
        def _(i=i):
            pl.semaphore_signal(barrier, inc=1, device_id=device[i], device_id_type=MESH)

    def slot_of(direction):
        k = jnp.int32(0)
        for x in range(1, FACES):
            k = jnp.where(dirs[0, 0, x] == direction, jnp.int32(x), k)
        return k

    slot = [slot_of(d) for d in ORDER]
    size = []
    for d in ORDER:
        n = sizes[0, 0, 0]
        for x in range(1, FACES):
            n = jnp.where(dirs[0, 0, x] == d, sizes[0, 0, x], n)
        size.append(n)

    def remote(buffer, into, send, recv, i, index):
        return pltpu.make_async_remote_copy(
            src_ref=buffer.at[(*index, i)], dst_ref=into.at[(*index, i ^ 1)],
            send_sem=send.at[(*index, i)], recv_sem=recv.at[(*index, i ^ 1)],
            device_id=device[i], device_id_type=MESH)

    def start(buffer, into, send, recv, i, index):
        @pl.when(exists[i])
        def _():
            remote(buffer, into, send, recv, i, index).start()

    def arrived(buffer, into, send, recv, i, index):
        @pl.when(exists[i])
        def _():
            pltpu.make_async_remote_copy(
                src_ref=buffer.at[(*index, i)], dst_ref=into.at[(*index, i)],
                send_sem=send.at[(*index, i)], recv_sem=recv.at[(*index, i)],
                device_id=device[i], device_id_type=MESH).wait_recv()

    def sent(buffer, into, send, recv, i, index):
        @pl.when(exists[i])
        def _():
            remote(buffer, into, send, recv, i, index).wait_send()

    corners = (corner, got_corner, corner_s, corner_r)
    pieces = (piece, got_piece, piece_s, piece_r)
    firsts = (load_send, got_load, load_s, load_r)
    faces = (face, got_face, face_s, face_r)

    for i in range(4):
        @pl.when(jnp.logical_not(exists[i]))
        def _(i=i):
            got_corner[i] = jnp.zeros((HALF + 8, HALF), F32)
            got_piece[i] = jnp.zeros((HALF, HALF), F32)
            got_load[i] = jnp.zeros((ROWS, HALF), F32)
            for j in range(2):
                got_face[j, i] = jnp.zeros((ROWS, HALF), F32)

    for i in range(4, FACES):
        got_face[1, i] = jnp.zeros((ROWS, HALF), F32)

    for c in fetch_diag:
        c.wait()
    fetch_load = []
    for k in range(FACES):
        fetch_load.append(pltpu.make_async_copy(
            loads.at[0, 0, pl.ds(k * ROWS, ROWS), :], load.at[k], dma.at[6 + k]))
        fetch_load[-1].start()
    fetch_full = []
    for k in range(FACES):
        for e in range(FACES):
            fetch_full.append(pltpu.make_async_copy(
                schur.at[0, 0, pl.ds(k * ROWS, ROWS), pl.ds(e * ROWS, ROWS)], full.at[k, e], full_s.at[k, e]))
            fetch_full[-1].start()

    hr = lax.broadcasted_iota(jnp.int32, (HALF, HALF), 0)
    hc = lax.broadcasted_iota(jnp.int32, (HALF, HALF), 1)
    parts = ((0, 0), (HALF, 0), (HALF, HALF))

    def own(j, i):
        r, c = parts[j]
        return diag[slot[i], pl.ds(r, HALF), pl.ds(c, HALF)]

    for i in range(4):
        first, last = own(0, i), own(2, i)
        corner[i, pl.ds(0, HALF), :] = jnp.where(hc <= hr, first, last)
        middle = jnp.sum(jnp.where(hc == hr, last, 0.0), axis=0, keepdims=True)
        corner[i, pl.ds(HALF, 8), :] = jnp.broadcast_to(middle, (8, HALF))
        piece[i] = own(1, i)

    count = jnp.int32(0)
    for e in exists:
        count = count + jnp.where(e, jnp.int32(1), jnp.int32(0))
    pl.semaphore_wait(barrier, count)
    for i in (2, 3, 0, 1):
        start(*corners, i, ())
    for c in fetch_load:
        c.wait()
    rowid = lax.broadcasted_iota(jnp.int32, (ROWS, HALF), 0)

    def masked(x, i):
        return jnp.where(rowid < size[i], x, 0.0)

    for i in range(FACES):
        x = masked(load[slot[i]], i)
        acc[i] = x
        if i < 4:
            load_send[i] = x

    def convert(half, s):
        part = ROWS // 4
        begin = pl.multiple_of(s * part, part)
        for i in range(3 * half, 3 * half + 3):
            for e in range(FACES):
                h, l = split(full[slot[i], slot[e], pl.ds(begin, part), :])
                both[pl.ds(i * 2 * ROWS + begin, part), pl.ds(e * ROWS, ROWS)] = h
                both[pl.ds(i * 2 * ROWS + ROWS + begin, part), pl.ds(e * ROWS, ROWS)] = l

    def assembled(j, i):
        r, c = parts[j]
        if i >= 4:
            x = own(j, i)
        elif j == 1:
            arrived(*pieces, i, ())
            x = piece[i] + got_piece[i]
        else:
            if j == 0:
                arrived(*corners, i, ())
            x = corner[i, pl.ds(0, HALF), :] + got_corner[i, pl.ds(0, HALF), :]
            x = jnp.where(hc <= hr if j == 0 else hc > hr, x, 0.0)
            y = x.T
            if j == 0:
                x = jnp.where(hc > hr, y, x)
            else:
                middle = corner[i, pl.ds(HALF, 8), :] + got_corner[i, pl.ds(HALF, 8), :]
                x = jnp.where(hc == hr, jnp.broadcast_to(middle[:1], (HALF, HALF)), x + y)
        x = jnp.where((hr + r < size[i]) & (hc + c < size[i]), x, 0.0)
        if r == c:
            x = jnp.where((hr == hc) & (hr + r >= size[i]), 1.0, x)
        return x

    def at(pair, i):
        return pair[i // 4].at[i % 4]

    def halve(i):
        p = rotate(at(top, i)[...], -i)
        at(top, i)[...] = p
        b = assembled(1, i)
        w = mm(b, p)
        cross[i] = w
        at(low, i)[...] = rotate(assembled(2, i) - mm(w, b.T), i)

    for c in fetch_full:
        c.wait()
    for i in (4, 5, 2, 3, 0, 1):
        at(top, i)[...] = rotate(assembled(0, i), i)
    for i in (2, 3, 0, 1):
        start(*pieces, i, ())

    for i in (2, 3, 0, 1):
        start(*firsts, i, ())

    def beside_top(s):
        convert(0, s)


    invert_halves(top, beside_top)
    for i in (4, 5, 2, 3, 0, 1):
        halve(i)
    invert_halves(low, functools.partial(convert, 1))

    def first_solve(i, r):
        p, w, q = at(top, i)[...], cross[i], rotate(at(low, i)[...], -i)
        at(low, i)[...] = q
        upper, lower = r[:HALF], r[HALF:]
        y = mm(q, lower - mm(w, upper))
        return OMEGA * jnp.concatenate([mm(p, upper) - mm(w.T, y), y], 0)

    def explicit(i):
        w, q = cross[i], at(low, i)[...]
        v = -mm(q, w)
        for r, c, x in ((0, 0, at(top, i)[...] - mm(w.T, v)), (HALF, 0, v), (0, HALF, v.T), (HALF, HALF, q)):
            h, l = split(x)
            inv[i, pl.ds(r, HALF), pl.ds(c, HALF)] = h
            inv[i, pl.ds(ROWS + r, HALF), pl.ds(c, HALF)] = l

    def folded(o):
        return (o[:ROWS, :HALF] + o[:ROWS, HALF:]) + (o[ROWS:, :HALF] + o[ROWS:, HALF:])

    def solve(i, r):
        h, l = split(r)
        w = jnp.concatenate([h, l], 1)
        return OMEGA * folded(jnp.dot(inv[i], w, preferred_element_type=F32))

    def keep(i, x):
        u[i] = x
        h, l = split(x)
        uu[pl.ds(i * ROWS, ROWS), pl.ds(0, HALF)] = h
        uu[pl.ds(i * ROWS, ROWS), pl.ds(HALF, HALF)] = l

    def applied(i, begin, end):
        rows, cols = pl.ds(i * 2 * ROWS, 4 * ROWS), pl.ds(begin * ROWS, (end - begin) * ROWS)
        o = jnp.dot(both[rows, cols], uu[cols, :], preferred_element_type=F32)
        return masked(folded(o[:2 * ROWS]), i), masked(folded(o[2 * ROWS:]), i + 1)

    for i in range(FACES):
        r = acc[i]
        if i < 4:
            arrived(*firsts, i, ())
            r = r + got_load[i]
        keep(i, first_solve(i, r))
    for i in range(0, FACES, 2):
        for j, x in enumerate(applied(i, 0, FACES)):
            face[0, i + j] = acc[i + j] - x
            if i < 4:
                start(*faces, i + j, (0,))

    for i in (4, 5, 2, 3, 0, 1):
        explicit(i)

    for i in (4, 5, 2, 3):
        r = face[0, i]
        if i < 4:
            arrived(*faces, i, (0,))
            r = r + got_face[0, i]
        keep(i, u[i] + solve(i, r))
    for i in range(0, FACES, 2):
        for j, x in enumerate(applied(i, 2, FACES)):
            acc[i + j] = acc[i + j] - x
    for i in (0, 1):
        arrived(*faces, i, (0,))
        keep(i, u[i] + solve(i, face[0, i] + got_face[0, i]))
    for i in (2, 0, 4):
        for j, x in enumerate(applied(i, 0, 2)):
            face[1, i + j] = acc[i + j] - x
            if i < 4:
                start(*faces, i + j, (1,))

    def place(k):
        d = dirs[0, 0, k]
        return jnp.where(d < 2, d + 2, jnp.where(d < 4, d - 2, d))

    gives = []

    def give(k, x, held, out, sems):
        rows = pl.ds(k * ROWS, ROWS)
        held[rows, :] = x
        gives.append(pltpu.make_async_copy(held.at[rows, :], out.at[0, 0, rows, :], sems.at[k]))
        gives[-1].start()

    for k in range(FACES):
        give(k, u[place(k)], out_disp, disp_out, disp_s)
    for i in range(4):
        arrived(*faces, i, (1,))
    for k in range(FACES):
        give(k, face[1, place(k)] + got_face[1, place(k)], out_resid, resid_out, resid_s)
    for i in range(4):
        sent(*corners, i, ())
        sent(*pieces, i, ())
        sent(*firsts, i, ())
        for j in range(2):
            sent(*faces, i, (j,))
    for c in gives:
        c.wait()


def hand_over(disp, resid, disp_out, resid_out, held, sems):
    rows = disp.shape[2] // 3
    ins, outs = [], []
    for i, (a, b) in enumerate(((disp, disp_out), (resid, resid_out))):
        for k in range(3):
            part = pl.ds(k * rows, rows)
            ins.append(pltpu.make_async_copy(a.at[0, 0, part, :], held.at[i, k], sems.at[0, i, k]))
            outs.append(pltpu.make_async_copy(held.at[i, k], b.at[0, 0, part, :], sems.at[1, i, k]))
            ins[-1].start()
    for c, d in zip(ins, outs):
        c.wait()
        d.start()
    for d in outs:
        d.wait()


def solution(mesh):
    grid = (mesh.shape["wide"], mesh.shape["depth"])

    def local(schur, loads, face_sizes, face_dir):
        order, cases = schur.shape[2], loads.shape[3]
        shape = jax.ShapeDtypeStruct((1, 1, order, cases), F32)
        hbm = pl.BlockSpec(memory_space=pl.ANY)
        smem = pl.BlockSpec(memory_space=pltpu.SMEM)
        vmem = pltpu.VMEM
        sem = pltpu.SemaphoreType.DMA
        found = pl.pallas_call(
            functools.partial(kernel, grid),
            out_shape=(shape, shape),
            in_specs=[hbm, hbm, smem, smem],
            out_specs=(hbm, hbm),
            scratch_shapes=[
                vmem((FACES, FACES, ROWS, ROWS), F32),
                vmem((FACES, ROWS, ROWS), F32),
                vmem((FACES, ROWS, HALF), F32),
                vmem((4, HALF + 8, HALF), F32),
                vmem((4, HALF + 8, HALF), F32),
                vmem((4, HALF, HALF), F32),
                vmem((4, HALF, HALF), F32),
                vmem((4, ROWS, HALF), F32),
                vmem((4, ROWS, HALF), F32),
                vmem((2, FACES, ROWS, HALF), F32),
                vmem((2, FACES, ROWS, HALF), F32),
                vmem((2 * order, order), BF16),
                vmem((4, HALF, HALF), F32),
                vmem((2, HALF, HALF), F32),
                vmem((4, HALF, HALF), F32),
                vmem((2, HALF, HALF), F32),
                vmem((FACES, HALF, HALF), F32),
                vmem((FACES, 2 * ROWS, ROWS), BF16),
                vmem((FACES, ROWS, HALF), F32),
                vmem((order, ROWS), BF16),
                vmem((FACES, ROWS, HALF), F32),
                vmem((order, cases), F32),
                vmem((order, cases), F32),
                sem((12,)),
                sem((FACES, FACES)),
                sem((FACES,)),
                sem((FACES,)),
                sem((4,)),
                sem((4,)),
                sem((4,)),
                sem((4,)),
                sem((4,)),
                sem((4,)),
                sem((2, 4)),
                sem((2, 4)),
            ],
            compiler_params=pltpu.CompilerParams(
                collective_id=0, has_side_effects=True, vmem_limit_bytes=56 << 20),
        )(schur, loads, face_sizes, face_dir)
        return tuple(pl.pallas_call(
            hand_over,
            out_shape=(shape, shape),
            in_specs=[hbm, hbm],
            out_specs=(hbm, hbm),
            scratch_shapes=[vmem((2, 3, order // 3, cases), F32), sem((2, 2, 3))],
        )(*found))

    return jax.shard_map(
        local,
        mesh=mesh,
        in_specs=(
            P("wide", "depth", None, None),
            P("wide", "depth", None, None),
            P("wide", "depth", None),
            P("wide", "depth", None),
        ),
        out_specs=(P("wide", "depth", None, None), P("wide", "depth", None, None)),
        check_vma=False,
    )
```
